256 devices in a mesh: row: 8 (over x, y_hi), col: 32 (over y_lo, z, core).
Axes of the slice: x: 4, y: 4 (y_hi: 2, y_lo: 2; y = y_hi * 2 + y_lo), z: 8, core: 2. Of those that a mesh axis runs over, the one named last changes fastest.
Arguments:
- queries: bfloat16 [32768, 1024], P(('row', 'col'))
- keys: bfloat16 [32768, 128], P(('row', 'col'))
- values: bfloat16 [32768, 128], P(('row', 'col')), may hold values from -6 to 6
- positions: int32 [32768], P(('row', 'col')), may hold values from 0 to 32767, each once
Outputs:
- attended: bfloat16 [32768, 1024], P(('row', 'col'))
- log_total: float32 [8, 32768], P(None, ('row', 'col'))
The draws below stay inside these ranges and needn't reach their ends.
Inputs may be any that keep to these rules, and one draw needn't show every extreme that they name: positions is a permutation of 0 to 32767.
All inputs are finite; a program needn't handle non-finite values.
Results may differ from the reference program's by a relative error of at most 0.015.
Values may be sent and summed in bfloat16 or wider, within the bound.
A program may use at most 64 MiB of HBM per device.

```python
import math
import jax
import jax.numpy as jnp
from jax import lax

HEADS = 8
HD = 128
TOK_DEV = 128
STEPS = 4
TOKENS = 32768
N_ROW = 8
N_COL = 32


def draw_queries(key, part):
    key = jax.random.fold_in(key, 1)
    result = 2.5 * jnp.clip(jax.random.normal(key, (TOKENS, HEADS * HD), jnp.float32), -6.0, 6.0)
    return result.astype(jnp.bfloat16)


def draw_keys(key, part):
    key = jax.random.fold_in(key, 2)
    result = jnp.clip(jax.random.normal(key, (TOKENS, HD), jnp.float32), -6.0, 6.0)
    return result.astype(jnp.bfloat16)


def level_of(key, dims, shards, smallest, top_value):
    gain = 1.0
    for position, blocks in shards:
        heights = jax.random.uniform(jax.random.fold_in(jax.random.fold_in(key, 6), position), (blocks,), jnp.float32, smallest / len(shards), top_value / len(shards))
        gain = gain * jnp.repeat(jnp.exp(heights), dims[position] // blocks).reshape((-1,) + (1,) * (len(dims) - 1 - position))
    return gain


def normal_values(stream_key, dims, width, most, split=(), kind=jnp.bfloat16):
    level = level_of(stream_key, dims, split, -0.22, 0.18) if split else 1.0
    array = jax.random.normal(stream_key, dims, jnp.float32) * width * level
    return jnp.minimum(jnp.maximum(array, -most), most).astype(kind)


def setup_inputs(seed: int = 0) -> dict:
    streams_of = jax.random.split(jax.random.key(seed), 5)
    return {
        "queries": draw_queries(jax.random.fold_in(streams_of[4], 71), 0),
        "keys": draw_keys(jax.random.fold_in(streams_of[4], 71), 0),
        "values": normal_values(streams_of[2], (TOKENS, HD), 1.0, 6.0, ((0, 256),)),
        "positions": jax.random.permutation(streams_of[3], TOKENS).astype(jnp.int32),
    }


MASKED_SCORE = -1.0e30


def reference(queries, keys, values, positions):
    group_tokens = TOK_DEV * N_COL
    block_rows = math.gcd(group_tokens, 512)
    block_count = TOKENS // block_rows
    score_scale = HD ** -0.5

    def attend_block(index):
        first = (index * block_rows).astype(jnp.int32)
        group = first // group_tokens
        query_block = lax.dynamic_slice_in_dim(queries, first, block_rows, 0).astype(jnp.float32)
        query_block = query_block.reshape(block_rows, HEADS, HD)
        query_place = lax.dynamic_slice_in_dim(positions, first, block_rows, 0)
        key_parts, value_parts, place_parts = [], [], []
        for visit in range(STEPS):
            anchor = (((group + visit) % N_ROW) * group_tokens).astype(jnp.int32)
            key_parts.append(lax.dynamic_slice_in_dim(keys, anchor, group_tokens, 0))
            value_parts.append(lax.dynamic_slice_in_dim(values, anchor, group_tokens, 0))
            place_parts.append(lax.dynamic_slice_in_dim(positions, anchor, group_tokens, 0))
        key_rows = jnp.concatenate(key_parts, 0).astype(jnp.float32)
        value_rows = jnp.concatenate(value_parts, 0).astype(jnp.float32)
        key_place = jnp.concatenate(place_parts, 0)
        scores = jnp.einsum("qhd,kd->hqk", query_block, key_rows) * score_scale
        visible = key_place[None, :] <= query_place[:, None]
        scores = jnp.where(visible[None], scores, MASKED_SCORE)
        top = jnp.max(scores, axis=-1)
        weights = jnp.where(visible[None], jnp.exp(scores - top[..., None]), 0.0)
        total = jnp.sum(weights, axis=-1)
        rounded = weights.astype(jnp.bfloat16).astype(jnp.float32)
        summed = jnp.einsum("hqk,kd->hqd", rounded, value_rows)
        output = (summed / total[..., None]).transpose(1, 0, 2).reshape(block_rows, HEADS * HD)
        return output.astype(jnp.bfloat16), top + jnp.log(total)

    outputs, totals = lax.map(attend_block, jnp.arange(block_count, dtype=jnp.int32))
    attended = outputs.reshape(TOKENS, HEADS * HD)
    log_total = totals.transpose(1, 0, 2).reshape(HEADS, TOKENS)
    return attended, log_total
```

```python
import functools
import math

import jax
import jax.numpy as jnp
from jax import lax
from jax.experimental import pallas as pl
from jax.experimental.pallas import tpu as pltpu
from jax.sharding import PartitionSpec as P

HEADS = 8
HD = 128
TOK = 128
GROUPS = 8
NZ = 8
BLOCK = 2 * HD + 16
TO_LOG2 = math.log2(math.e) / math.sqrt(HD)
LN2 = math.log(2.0)
HIDDEN = -(2.0**100)
START = -1e30
ITEMS = 10

MESH = pl.DeviceIdType.MESH
F32 = jnp.float32
BF16 = jnp.bfloat16


def column_of(row_vector):
    return jnp.broadcast_to(row_vector, (TOK, TOK)).T


def kernel(
    q_ref, k_ref, v_ref, pos_ref, att_ref, log_ref,
    blocks, queries, places, place_out, place_in, eye, acc, top,
    part_out, part_in, lse_out, lse_in,
    col_send, col_recv, up_send, up_recv, down_send, down_recv, sib_send, sib_recv,
    q_send, q_recv, back_send, back_recv,
):
    row = lax.axis_index("row")
    col = lax.axis_index("col")
    lo = col // 16
    z = (col // 2) % NZ
    core = col % 2

    def place(lo_, z_, core_):
        return lo_ * 16 + z_ * 2 + core_

    partner = (row, place(1 - lo, z, core))
    sibling = (row, place(lo, z, 1 - core))
    above = (row, place(lo, (z + 1) % NZ, core))
    below = (row, place(lo, (z + NZ - 1) % NZ, core))
    before = (row + GROUPS - 1) % GROUPS
    after = (row + 1) % GROUPS
    before_at = [(before, place(l, z, core)) for l in range(2)]
    after_at = [(after, place(l, z, core)) for l in range(2)]
    queries_to = ((row + 2) % GROUPS, col)
    queries_from = ((row + GROUPS - 2) % GROUPS, col)

    barrier = pltpu.get_barrier_semaphore()
    partners = [partner, sibling, above, below, *before_at, *after_at, queries_to, queries_from]
    for device in partners:
        pl.semaphore_signal(barrier, inc=1, device_id=device, device_id_type=MESH)

    own = blocks.at[core, z, lo]
    own[0:HD, :] = k_ref[...].astype(F32).T.astype(BF16)
    own[HD : 2 * HD, :] = v_ref[...]
    pos = pos_ref[...]
    high, low = (pos // 256).astype(F32), (pos % 256).astype(F32)
    line = lax.broadcasted_iota(jnp.int32, (16, TOK), 0)
    coded = jnp.where(line == 0, high, jnp.where(line == 1, low, 0.0)).astype(BF16)
    own[2 * HD : BLOCK, :] = coded
    place_out[...] = coded
    queries[0] = q_ref[...]
    places[0] = column_of(high * 256.0 + low)
    eye[...] = (
        lax.broadcasted_iota(jnp.int32, (TOK, TOK), 0) == lax.broadcasted_iota(jnp.int32, (TOK, TOK), 1)
    ).astype(BF16)
    acc[...] = jnp.zeros_like(acc)
    top[...] = jnp.full_like(top, START)

    pl.semaphore_wait(barrier, len(partners))

    def remote(src, dst, send, recv, device):
        return pltpu.make_async_remote_copy(
            src_ref=src, dst_ref=dst, send_sem=send, recv_sem=recv, device_id=device, device_id_type=MESH
        )

    def column_copy(number, device, slot):
        return remote(own, blocks.at[core, z, slot], col_send.at[number], col_recv.at[slot], device)

    column = [
        column_copy(0, partner, lo),
        column_copy(1, before_at[0], 2 + lo),
        column_copy(2, before_at[1], 2 + lo),
    ]
    for copy in column:
        copy.start()
    send_places = remote(place_out, place_in, q_send.at[0], q_recv.at[0], queries_to)
    send_queries = remote(q_ref, queries.at[1], q_send.at[1], q_recv.at[1], queries_to)
    send_places.start()
    send_queries.start()

    def z_at(distance):
        return (z + NZ + distance) % NZ

    def ring(step, up):
        bundle = z_at(-step if up else step)
        part = blocks.at[core, bundle]
        if step == 3:
            part = part.at[pl.ds(0, 2)] if up else part.at[pl.ds(2, 2)]
        if up:
            return remote(part, part, up_send.at[step], up_recv.at[step], above)
        return remote(part, part, down_send.at[step], down_recv.at[step], below)

    def arrived(step, up):
        bundle = z_at(-(step + 1) if up else step + 1)
        part = blocks.at[core, bundle]
        if step == 3:
            part = part.at[pl.ds(0, 2)] if up else part.at[pl.ds(2, 2)]
        if up:
            remote(part, part, up_send.at[step], up_recv.at[step], above).wait_recv()
        else:
            remote(part, part, down_send.at[step], down_recv.at[step], below).wait_recv()

    def across(number, distance):
        part = blocks.at[core, z_at(distance)]
        return remote(part, part, sib_send.at[number], sib_recv.at[number], sibling)

    def from_sibling(number, distance):
        part = blocks.at[1 - core, z_at(distance)]
        remote(part, part, sib_send.at[number], sib_recv.at[number], sibling).wait_recv()

    for slot, device in ((1 - lo, partner), (2, after_at[0]), (3, after_at[1])):
        remote(own, blocks.at[core, z, slot], col_send.at[0], col_recv.at[slot], device).wait_recv()
    ring(0, True).start()
    ring(0, False).start()
    across(0, 0).start()
    from_sibling(0, 0)

    def attend(which, spots):
        parts = [blocks.at[c, spot, j] for spot in spots for c in range(2) for j in range(4)]
        count = len(parts)
        keys = jnp.concatenate([part[0:HD, :] for part in parts], axis=1)
        values = jnp.concatenate([part[HD : 2 * HD, :] for part in parts], axis=0)
        values = jnp.concatenate([values, jnp.ones((count * TOK, HD), BF16)], axis=1)
        own_place = places[which]
        bias = []
        for part in parts:
            key_place = part[2 * HD : 2 * HD + 1, :].astype(F32) * 256.0 + part[2 * HD + 1 : 2 * HD + 2, :].astype(F32)
            bias.append(jnp.where(key_place <= own_place, 0.0, HIDDEN).astype(BF16))
        keys = jnp.concatenate([keys, jnp.concatenate(bias, axis=1)], axis=0)
        for head in range(HEADS):
            rows = pl.ds(head * TOK, TOK)
            left = jnp.concatenate([queries[which, :, head * HD : (head + 1) * HD], eye[...]], axis=1)
            scores = jnp.dot(left, keys, preferred_element_type=F32)
            most = scores[:, 0:TOK]
            for i in range(1, count):
                most = jnp.maximum(most, scores[:, i * TOK : (i + 1) * TOK])
            old = top[which, rows, :]
            new = jnp.maximum(old, jnp.max(most, axis=1, keepdims=True) * TO_LOG2)
            fade = jnp.exp2(old - new)
            top[which, rows, :] = new
            weights = jnp.concatenate(
                [jnp.exp2(scores[:, i * TOK : (i + 1) * TOK] * TO_LOG2 - new).astype(BF16) for i in range(count)],
                axis=1,
            )
            acc[which, rows, :] = acc[which, rows, :] * jnp.concatenate([fade, fade], axis=1) + jnp.dot(
                weights, values, preferred_element_type=F32
            )

    def item(i, carry):
        other = (i == 1) | (i == 2) | (i == 4) | (i == 6) | (i == 7)
        which = jnp.where(other, 1, 0)
        distance = jnp.where(i < 7, i // 2, jnp.where(i == 8, 3, 4))

        @pl.when(i == 1)
        def _():
            send_places.wait_recv()
            send_queries.wait_recv()
            got = place_in[...].astype(F32)
            places[1] = column_of(got[0:1, :] * 256.0 + got[1:2, :])

        for step in range(3):

            @pl.when(i == 2 * step + 2)
            def _(step=step):
                arrived(step, True)
                ring(step + 1, True).start()
                across(2 * step + 1, -(step + 1)).start()
                arrived(step, False)
                ring(step + 1, False).start()
                across(2 * step + 2, step + 1).start()
                from_sibling(2 * step + 1, -(step + 1))
                from_sibling(2 * step + 2, step + 1)

        @pl.when(i == 7)
        def _():
            arrived(3, True)
            arrived(3, False)
            across(7, 4).start()
            from_sibling(7, 4)

        single = (distance == 0) | (distance == 4)

        @pl.when(single)
        def _():
            attend(which, [(z + distance) % NZ])

        @pl.when(jnp.logical_not(single))
        def _():
            attend(which, [(z + NZ - distance) % NZ, (z + distance) % NZ])

        @pl.when(i == 7)
        def _():
            for head in range(HEADS):
                rows = pl.ds(head * TOK, TOK)
                total = acc[1, rows, HD:]
                part_out[rows, :] = (acc[1, rows, 0:HD] / total).astype(BF16)
                lse = top[1, rows, :] + jnp.log2(total)
                lse_out[head : head + 1, :] = jnp.sum(jnp.where(eye[...] != 0, lse, 0.0), axis=0, keepdims=True)
            remote(part_out, part_in, back_send.at[0], back_recv.at[0], queries_from).start()
            remote(lse_out, lse_in, back_send.at[1], back_recv.at[1], queries_from).start()

        return carry

    lax.fori_loop(0, ITEMS, item, 0)

    part_back = remote(part_out, part_in, back_send.at[0], back_recv.at[0], queries_from)
    lse_back = remote(lse_out, lse_in, back_send.at[1], back_recv.at[1], queries_from)
    lse_back.wait_recv()
    part_back.wait_recv()
    for head in range(HEADS):
        rows = pl.ds(head * TOK, TOK)
        total = acc[0, rows, HD:]
        mine = top[0, rows, :] + jnp.log2(total)
        theirs = column_of(lse_in[head : head + 1, :])
        larger = jnp.maximum(mine, theirs)
        share, other_share = jnp.exp2(mine - larger), jnp.exp2(theirs - larger)
        both = share + other_share
        result = acc[0, rows, 0:HD] * (share / (total * both)) + part_in[rows, :].astype(F32) * (other_share / both)
        att_ref[:, head * HD : (head + 1) * HD] = result.astype(BF16)
        lse = (larger + jnp.log2(both)) * LN2
        log_ref[head : head + 1, :] = jnp.sum(jnp.where(eye[...] != 0, lse, 0.0), axis=0, keepdims=True)

    for copy in column:
        copy.wait_send()
    send_places.wait_send()
    send_queries.wait_send()
    for step in range(4):
        ring(step, True).wait_send()
        ring(step, False).wait_send()
    across(0, 0).wait_send()
    for step in range(3):
        across(2 * step + 1, -(step + 1)).wait_send()
        across(2 * step + 2, step + 1).wait_send()
    across(7, 4).wait_send()
    part_back.wait_send()
    lse_back.wait_send()


def local(queries, keys, values, positions):
    vmem = pl.BlockSpec(memory_space=pltpu.VMEM)
    dma = pltpu.SemaphoreType.DMA
    return pl.pallas_call(
        kernel,
        out_shape=(
            jax.ShapeDtypeStruct((TOK, HEADS * HD), BF16),
            jax.ShapeDtypeStruct((HEADS, TOK), F32),
        ),
        in_specs=[vmem] * 4,
        out_specs=(vmem, vmem),
        scratch_shapes=[
            pltpu.VMEM((2, NZ, 4, BLOCK, HD), BF16),
            pltpu.VMEM((2, TOK, HEADS * HD), BF16),
            pltpu.VMEM((2, TOK, TOK), F32),
            pltpu.VMEM((16, TOK), BF16),
            pltpu.VMEM((16, TOK), BF16),
            pltpu.VMEM((TOK, TOK), BF16),
            pltpu.VMEM((2, HEADS * TOK, 2 * HD), F32),
            pltpu.VMEM((2, HEADS * TOK, TOK), F32),
            pltpu.VMEM((HEADS * TOK, HD), BF16),
            pltpu.VMEM((HEADS * TOK, HD), BF16),
            pltpu.VMEM((HEADS, TOK), F32),
            pltpu.VMEM((HEADS, TOK), F32),
            dma((3,)), dma((4,)),
            dma((4,)), dma((4,)), dma((4,)), dma((4,)),
            dma((8,)), dma((8,)),
            dma((2,)), dma((2,)), dma((2,)), dma((2,)),
        ],
        compiler_params=pltpu.CompilerParams(
            collective_id=0, has_side_effects=True, vmem_limit_bytes=48 * 2**20
        ),
    )(queries, keys, values, positions.reshape(1, TOK))


def solution(mesh):
    placed = (
        P(("row", "col"), None),
        P(("row", "col"), None),
        P(("row", "col"), None),
        P(("row", "col")),
    )
    return jax.shard_map(
        local,
        mesh=mesh,
        in_specs=placed,
        out_specs=(P(("row", "col"), None), P(None, ("row", "col"))),
        check_vma=False,
    )
```

```python
import functools
import math

import jax
import jax.numpy as jnp
from jax import lax
from jax.experimental import pallas as pl
from jax.experimental.pallas import tpu as pltpu
from jax.sharding import PartitionSpec as P

HEADS = 8
HD = 128
TOK = 128
GROUPS = 8
NZ = 8
BLOCK = 2 * HD + 16
TO_LOG2 = math.log2(math.e) / math.sqrt(HD)
LN2 = math.log(2.0)
HIDDEN = -(2.0**100)
START = -1e30
ITEMS = 10
BACK_ROWS = 256
OFFSETS = (0, 1, -1, 2, -2, 3, -3, 4)
HALF = 144
SMALL = (
    ((0, 0), (1, 0), (2, 0), (0, 1)),
    ((2, 7), (3, 7), (3, 5), (3, 6)),
)
LARGE = (
    ((0, 2), (3, 0), (1, 1), (1, 2), (2, 1), (2, 2), (0, 3), (0, 4)),
    ((3, 1), (3, 2), (1, 3), (1, 4), (2, 3), (2, 4), (0, 5), (0, 6)),
    ((3, 3), (3, 4), (1, 5), (1, 6), (2, 5), (2, 6), (0, 7), (1, 7)),
)

MESH = pl.DeviceIdType.MESH
F32 = jnp.float32
BF16 = jnp.bfloat16


def column_of(row_vector):
    return jnp.broadcast_to(row_vector, (TOK, TOK)).T


def kernel(
    q_hbm, k_hbm, v_hbm, pos_hbm, att_ref, log_ref,
    blocks, queries, key_in, pos_in, places, place_out, place_in, eye, acc, top,
    part_out, part_in, lse_out, lse_in,
    load, z_send, half_recv, column_send, line_recv, partner_send, near_send, far_send, sib_send, sib_recv,
    q_send, q_recv, back_send, back_recv, lse_send, lse_recv,
):
    row = lax.axis_index("row")
    col = lax.axis_index("col")
    lo = col // 16
    z = (col // 2) % NZ
    core = col % 2

    def spot(distance):
        return (z + NZ + distance) % NZ

    def at(row_, lo_, z_, core_):
        return ((row_ + GROUPS) % GROUPS, lo_ * 16 + z_ * 2 + core_)

    partner = at(row, 1 - lo, z, core)
    sibling = at(row, lo, z, 1 - core)
    near_before = at(row - 2, lo, z, core)
    near_after = at(row + 2, lo, z, core)
    queries_to = at(row + 1, 1 - lo, z, core)
    queries_from = at(row - 1, 1 - lo, z, core)
    along_z = {d: at(row, lo, spot(d), core) for d in (1, -1, 2, -2)}

    own = blocks.at[core, z, 0]
    loads = [
        pltpu.make_async_copy(k_hbm, key_in, load.at[0]),
        pltpu.make_async_copy(v_hbm, own.at[pl.ds(HD, HD)], load.at[1]),
        pltpu.make_async_copy(pos_hbm, pos_in, load.at[2]),
        pltpu.make_async_copy(q_hbm, queries.at[0], load.at[3]),
    ]
    for copy in loads:
        copy.start()

    barrier = pltpu.get_barrier_semaphore()
    partners = [partner, sibling, near_before, near_after, queries_to, queries_from, *along_z.values()]
    for device in partners:
        pl.semaphore_signal(barrier, inc=1, device_id=device, device_id_type=MESH)

    eye[...] = (
        lax.broadcasted_iota(jnp.int32, (TOK, TOK), 0) == lax.broadcasted_iota(jnp.int32, (TOK, TOK), 1)
    ).astype(BF16)
    acc[...] = jnp.zeros_like(acc)
    top[...] = jnp.full_like(top, START)
    for copy in loads:
        copy.wait()

    own[0:HD, :] = key_in[...].astype(F32).T.astype(BF16)
    pos = pos_in[...]
    high, low = (pos // 256).astype(F32), (pos % 256).astype(F32)
    line = lax.broadcasted_iota(jnp.int32, (16, TOK), 0)
    coded = jnp.where(line == 0, high, jnp.where(line == 1, low, 0.0)).astype(BF16)
    own[2 * HD : BLOCK, :] = coded
    place_out[...] = coded
    places[0] = column_of(high * 256.0 + low)

    pl.semaphore_wait(barrier, len(partners))

    def remote(src, dst, send, recv, device):
        return pltpu.make_async_remote_copy(
            src_ref=src, dst_ref=dst, send_sem=send, recv_sem=recv, device_id=device, device_id_type=MESH
        )

    def block(line_, e, core_=None):
        return blocks.at[core if core_ is None else core_, spot(OFFSETS[e]), line_]

    def z_copy(n):
        d = (1, -1, 2, -2, 1, -1, 2, -2)[n]
        if n < 4:
            return remote(own, own, z_send.at[n], line_recv.at[0, OFFSETS.index(-d)], along_z[d])
        came = -2 if d > 0 else 2
        ref = block(0, OFFSETS.index(came))
        if n < 6:
            return remote(ref, ref, z_send.at[n], line_recv.at[0, OFFSETS.index(came - d)], along_z[d])
        ref = ref.at[pl.ds(0, HALF)] if d > 0 else ref.at[pl.ds(HALF, BLOCK - HALF)]
        return remote(ref, ref, z_send.at[n], half_recv.at[n - 6], along_z[d])

    def column_copy(n):
        d = (1, -1)[n % 2]
        ref = blocks.at[core, z, pl.ds(1, 2) if n < 2 else pl.ds(3, 1)]
        return remote(ref, ref, column_send.at[n], line_recv.at[1 if n < 2 else 3, OFFSETS.index(-d)], along_z[d])

    def partner_copy(e):
        return remote(block(0, e), block(2, e), partner_send.at[e], line_recv.at[2, e], partner)

    def near_copy(e):
        return remote(block(0, e), block(1, e), near_send.at[e], line_recv.at[1, e], near_before)

    far_to = tuple(jnp.where(core == 0, p, n) for p, n in zip(partner, near_before))

    def far_copy(e):
        return remote(block(1 + core, e), block(3, e), far_send.at[e], line_recv.at[3, e], far_to)

    def sib_copy(part, e, core_=None):
        first, count = ((0, 1), (1, 2), (3, 1))[part]
        ref = blocks.at[core if core_ is None else core_, spot(OFFSETS[e]), pl.ds(first, count)]
        return remote(ref, ref, sib_send.at[part, e], sib_recv.at[part, e], sibling)

    def arrived(line_, e):
        if line_ == 0 and e == 7:
            for n in range(2):
                z_copy(6 + n).wait_recv()
            return
        ref = block(line_, e)
        if line_ == 1 and e in (1, 2):
            ref = blocks.at[core, spot(OFFSETS[e]), pl.ds(1, 2)]
        remote(ref, ref, z_send.at[0], line_recv.at[line_, e], sibling).wait_recv()

    def pass_on(e):
        if e > 0:
            arrived(0, e)
        if e == 4:
            z_copy(4).start()
            z_copy(6).start()
        if e == 3:
            z_copy(5).start()
            z_copy(7).start()
        if e not in (1, 2):
            partner_copy(e).start()
            near_copy(e).start()
        sib_copy(0, e).start()

    def pass_far(e):
        arrived(1, e)
        if e not in (1, 2):
            arrived(2, e)
            far_copy(e).start()
        if e == 0:
            column_copy(0).start()
            column_copy(1).start()
        sib_copy(1, e).start()

    def pass_last(e):
        arrived(3, e)
        if e == 0:
            column_copy(2).start()
            column_copy(3).start()
        sib_copy(2, e).start()

    def from_sibling(part, e):
        sib_copy(part, e, 1 - core).wait_recv()

    def need(messages):
        for part, e in messages:
            from_sibling(part, e)

    for n in (0, 1):
        z_copy(n).start()
    pass_on(0)
    send_places = remote(place_out, place_in, q_send.at[0], q_recv.at[0], queries_to)
    send_queries = remote(queries.at[0], queries.at[1], q_send.at[1], q_recv.at[1], queries_to)
    for n in (2, 3):
        z_copy(n).start()
    send_places.start()
    send_queries.start()
    pass_far(0)
    pass_on(1)
    pass_on(2)
    need(((0, 0), (0, 1), (1, 0)))

    def attend(which, spots):
        parts = [blocks.at[c, zz, j] for zz, j in spots for c in range(2)]
        count = len(parts)
        keys = jnp.concatenate([part[0:HD, :] for part in parts], axis=1)
        values = jnp.concatenate([part[HD : 2 * HD, :] for part in parts], axis=0)
        values = jnp.concatenate([values, jnp.ones((count * TOK, HD), BF16)], axis=1)
        own_place = places[which]
        bias = []
        for part in parts:
            key_place = part[2 * HD : 2 * HD + 1, :].astype(F32) * 256.0 + part[2 * HD + 1 : 2 * HD + 2, :].astype(F32)
            bias.append(jnp.where(key_place <= own_place, 0.0, HIDDEN).astype(BF16))
        keys = jnp.concatenate([keys, jnp.concatenate(bias, axis=1)], axis=0)
        for head in range(HEADS):
            rows = pl.ds(head * TOK, TOK)
            left = jnp.concatenate([queries[which, :, head * HD : (head + 1) * HD], eye[...]], axis=1)
            scores = jnp.dot(left, keys, preferred_element_type=F32)
            most = scores[:, 0:TOK]
            for i in range(1, count):
                most = jnp.maximum(most, scores[:, i * TOK : (i + 1) * TOK])
            old = top[which, rows, :]
            new = jnp.maximum(old, jnp.max(most, axis=1, keepdims=True) * TO_LOG2)
            fade = jnp.exp2(old - new)
            top[which, rows, :] = new
            weights = jnp.concatenate(
                [jnp.exp2(scores[:, i * TOK : (i + 1) * TOK] * TO_LOG2 - new).astype(BF16) for i in range(count)],
                axis=1,
            )
            acc[which, rows, :] = acc[which, rows, :] * jnp.concatenate([fade, fade], axis=1) + jnp.dot(
                weights, values, preferred_element_type=F32
            )

    def back_copy(n):
        rows = pl.ds(n * BACK_ROWS, BACK_ROWS)
        return remote(part_out.at[rows], part_in.at[rows], back_send.at[n], back_recv.at[n], queries_from)

    lse_copy = remote(lse_out, lse_in, lse_send.at[0], lse_recv.at[0], queries_from)

    def early(i):
        if i == 1:
            pass_last(0)
            pass_on(3)
            pass_on(4)
            send_places.wait_recv()
            send_queries.wait_recv()
            got = place_in[...].astype(F32)
            places[1] = column_of(got[0:1, :] * 256.0 + got[1:2, :])
        elif i == 2:
            pass_far(1)
            pass_far(2)
            need(((0, 2), (2, 0), (1, 1), (1, 2), (0, 3), (0, 4)))
        elif i == 3:
            pass_on(5)
            pass_on(6)
            pass_last(1)
            pass_last(2)
            pass_far(3)
            pass_far(4)
        elif i == 4:
            pass_on(7)
            need(((2, 1), (2, 2), (1, 3), (1, 4), (0, 5), (0, 6)))
        elif i == 5:
            pass_far(5)
            pass_far(6)
            pass_far(7)
            pass_last(3)
            pass_last(4)
        elif i == 6:
            need(((2, 3), (2, 4), (1, 5), (1, 6), (0, 7), (1, 7)))
            pass_last(5)
            pass_last(6)
            pass_last(7)
        elif i == 7:
            need(((2, 7), (2, 5), (2, 6)))

    def give_back():
        for head in range(HEADS):
            rows = pl.ds(head * TOK, TOK)
            total = acc[1, rows, HD:]
            part_out[rows, :] = (acc[1, rows, 0:HD] / total).astype(BF16)
            if (head + 1) * TOK % BACK_ROWS == 0:
                back_copy((head + 1) * TOK // BACK_ROWS - 1).start()
            lse = top[1, rows, :] + jnp.log2(total)
            lse_out[head : head + 1, :] = jnp.sum(jnp.where(eye[...] != 0, lse, 0.0), axis=0, keepdims=True)
        lse_copy.start()

    def choose(index, tiles):
        found = []
        for choices in zip(*tiles):
            line_, distance = choices[-1][0], OFFSETS[choices[-1][1]]
            for n in range(len(tiles) - 1):
                line_ = jnp.where(index == n, choices[n][0], line_)
                distance = jnp.where(index == n, OFFSETS[choices[n][1]], distance)
            found.append((spot(distance), line_))
        return found

    def item(i, carry):
        other = (i == 1) | (i == 2) | (i == 4) | (i == 6) | (i == 7)
        which = jnp.where(other, 1, 0)
        for n in range(1, 8):

            @pl.when(i == n)
            def _(n=n):
                early(n)

        small = (i < 2) | (i == 7) | (i == 9)

        @pl.when(small)
        def _():
            attend(which, choose(jnp.where(i < 2, 0, 1), SMALL))

        @pl.when(jnp.logical_not(small))
        def _():
            attend(which, choose(jnp.where(i == 8, 2, i // 2 - 1), LARGE))

        @pl.when(i == 7)
        def _():
            give_back()

        return carry

    lax.fori_loop(0, ITEMS, item, 0)

    lse_copy.wait_recv()
    for head in range(HEADS):
        rows = pl.ds(head * TOK, TOK)
        if head * TOK % BACK_ROWS == 0:
            back_copy(head * TOK // BACK_ROWS).wait_recv()
        total = acc[0, rows, HD:]
        mine = top[0, rows, :] + jnp.log2(total)
        theirs = column_of(lse_in[head : head + 1, :])
        larger = jnp.maximum(mine, theirs)
        share, other_share = jnp.exp2(mine - larger), jnp.exp2(theirs - larger)
        both = share + other_share
        result = acc[0, rows, 0:HD] * (share / (total * both)) + part_in[rows, :].astype(F32) * (other_share / both)
        att_ref[:, head * HD : (head + 1) * HD] = result.astype(BF16)
        lse = (larger + jnp.log2(both)) * LN2
        log_ref[head : head + 1, :] = jnp.sum(jnp.where(eye[...] != 0, lse, 0.0), axis=0, keepdims=True)

    for n in range(8):
        z_copy(n).wait_send()
    for n in range(4):
        column_copy(n).wait_send()
    for e in range(NZ):
        if e not in (1, 2):
            partner_copy(e).wait_send()
            near_copy(e).wait_send()
            far_copy(e).wait_send()
        for part in range(3):
            sib_copy(part, e).wait_send()
    send_places.wait_send()
    send_queries.wait_send()
    for n in range(HEADS * TOK // BACK_ROWS):
        back_copy(n).wait_send()
    lse_copy.wait_send()


def local(queries, keys, values, positions):
    vmem = pl.BlockSpec(memory_space=pltpu.VMEM)
    hbm = pl.BlockSpec(memory_space=pltpu.HBM)
    dma = pltpu.SemaphoreType.DMA
    backs = HEADS * TOK // BACK_ROWS
    return pl.pallas_call(
        kernel,
        out_shape=(
            jax.ShapeDtypeStruct((TOK, HEADS * HD), BF16),
            jax.ShapeDtypeStruct((HEADS, TOK), F32),
        ),
        in_specs=[hbm] * 4,
        out_specs=(vmem, vmem),
        scratch_shapes=[
            pltpu.VMEM((2, NZ, 4, BLOCK, HD), BF16),
            pltpu.VMEM((2, TOK, HEADS * HD), BF16),
            pltpu.VMEM((TOK, HD), BF16),
            pltpu.VMEM((1, TOK), jnp.int32),
            pltpu.VMEM((2, TOK, TOK), F32),
            pltpu.VMEM((16, TOK), BF16),
            pltpu.VMEM((16, TOK), BF16),
            pltpu.VMEM((TOK, TOK), BF16),
            pltpu.VMEM((2, HEADS * TOK, 2 * HD), F32),
            pltpu.VMEM((2, HEADS * TOK, TOK), F32),
            pltpu.VMEM((HEADS * TOK, HD), BF16),
            pltpu.VMEM((HEADS * TOK, HD), BF16),
            pltpu.VMEM((HEADS, TOK), F32),
            pltpu.VMEM((HEADS, TOK), F32),
            dma((4,)), dma((8,)), dma((2,)), dma((4,)), dma((4, NZ)), dma((NZ,)), dma((NZ,)), dma((NZ,)), dma((3, NZ)), dma((3, NZ)),
            dma((2,)), dma((2,)), dma((backs,)), dma((backs,)), dma((1,)), dma((1,)),
        ],
        compiler_params=pltpu.CompilerParams(
            collective_id=0, has_side_effects=True, vmem_limit_bytes=63 * 2**20
        ),
    )(queries, keys, values, positions.reshape(1, TOK))


def solution(mesh):
    placed = (
        P(("row", "col"), None),
        P(("row", "col"), None),
        P(("row", "col"), None),
        P(("row", "col")),
    )
    return jax.shard_map(
        local,
        mesh=mesh,
        in_specs=placed,
        out_specs=(P(("row", "col"), None), P(None, ("row", "col"))),
        check_vma=False,
    )
```

```python
import functools
import math

import jax
import jax.numpy as jnp
from jax import lax
from jax.experimental import pallas as pl
from jax.experimental.pallas import tpu as pltpu
from jax.sharding import PartitionSpec as P

HEADS = 8
HD = 128
TOK = 128
GROUPS = 8
NZ = 8
BLOCK = 2 * HD + 16
TO_LOG2 = math.log2(math.e) / math.sqrt(HD)
LN2 = math.log(2.0)
HIDDEN = -(2.0**100)
START = -1e30
ITEMS = 12
BACK_ROWS = 256
OFFSETS = (0, 1, -1, 2, -2, 3, -3, 4)
HALF = 144
DIRECT = (7,)
STAGES = (
    ((0, 0), (1, 0), (2, 0), (0, 1)),
    ((0, 2), (3, 0), (1, 1), (1, 2), (2, 1), (2, 2), (0, 3), (0, 4)),
    ((3, 1), (3, 2), (1, 3), (1, 4), (2, 3), (2, 4), (0, 5), (0, 6)),
    ((3, 3), (3, 4), (1, 5), (1, 6), (2, 5), (2, 6), (0, 7), (1, 7)),
    ((2, 7), (3, 7), (3, 5), (3, 6)),
)


def tile(own_stage, other_stage):
    own = STAGES[own_stage] if own_stage is not None else ()
    other = STAGES[other_stage] if other_stage is not None else ()
    return tuple((0, *b) for b in own) + tuple((1, *b) for b in other)


SMALL = (tile(0, None), tile(None, 4))
MIDDLE = (tile(1, 0), tile(4, 3))
LARGE = (tile(2, 1), tile(3, 2))

MESH = pl.DeviceIdType.MESH
F32 = jnp.float32
BF16 = jnp.bfloat16


def column_of(row_vector):
    return jnp.broadcast_to(row_vector, (TOK, TOK)).T


def kernel(
    q_hbm, k_hbm, v_hbm, pos_hbm, att_ref, log_ref,
    blocks, queries, key_in, pos_in, places, place_out, place_in, eye, acc, top,
    part_out, part_in, lse_out, lse_in,
    load, z_send, half_recv, column_send, line_recv, partner_send, near_send, far_send, sib_send, sib_recv,
    q_send, q_recv, back_send, back_recv, lse_send, lse_recv,
):
    row = lax.axis_index("row")
    col = lax.axis_index("col")
    lo = col // 16
    z = (col // 2) % NZ
    core = col % 2

    def spot(distance):
        return (z + NZ + distance) % NZ

    def at(row_, lo_, z_, core_):
        return ((row_ + GROUPS) % GROUPS, lo_ * 16 + z_ * 2 + core_)

    partner = at(row, 1 - lo, z, core)
    sibling = at(row, lo, z, 1 - core)
    near_before = at(row - 2, lo, z, core)
    near_after = at(row + 2, lo, z, core)
    far_before = at(row - 2, 1 - lo, z, core)
    far_after = at(row + 2, 1 - lo, z, core)
    queries_to = at(row + 1, 1 - lo, z, core)
    queries_from = at(row - 1, 1 - lo, z, core)
    along_z = {d: at(row, lo, spot(d), core) for d in (1, -1, 2, -2)}

    own = blocks.at[core, z, 0]
    loads = [
        pltpu.make_async_copy(k_hbm, key_in, load.at[0]),
        pltpu.make_async_copy(v_hbm, own.at[pl.ds(HD, HD)], load.at[1]),
        pltpu.make_async_copy(pos_hbm, pos_in, load.at[2]),
        pltpu.make_async_copy(q_hbm, queries.at[0], load.at[3]),
    ]
    for copy in loads:
        copy.start()

    barrier = pltpu.get_barrier_semaphore()
    partners = [partner, sibling, near_before, near_after, far_before, far_after, queries_to, queries_from, *along_z.values()]
    for device in partners:
        pl.semaphore_signal(barrier, inc=1, device_id=device, device_id_type=MESH)

    eye[...] = (
        lax.broadcasted_iota(jnp.int32, (TOK, TOK), 0) == lax.broadcasted_iota(jnp.int32, (TOK, TOK), 1)
    ).astype(BF16)
    acc[...] = jnp.zeros_like(acc)
    top[...] = jnp.full_like(top, START)
    for copy in loads:
        copy.wait()

    own[0:HD, :] = key_in[...].astype(F32).T.astype(BF16)
    pos = pos_in[...]
    high, low = (pos // 256).astype(F32), (pos % 256).astype(F32)
    line = lax.broadcasted_iota(jnp.int32, (16, TOK), 0)
    coded = jnp.where(line == 0, high, jnp.where(line == 1, low, 0.0)).astype(BF16)
    own[2 * HD : BLOCK, :] = coded
    place_out[...] = coded
    places[0] = column_of(high * 256.0 + low)

    pl.semaphore_wait(barrier, len(partners))

    def remote(src, dst, send, recv, device):
        return pltpu.make_async_remote_copy(
            src_ref=src, dst_ref=dst, send_sem=send, recv_sem=recv, device_id=device, device_id_type=MESH
        )

    def block(line_, e, core_=None):
        return blocks.at[core if core_ is None else core_, spot(OFFSETS[e]), line_]

    def z_copy(n):
        d = (1, -1, 2, -2, 1, -1, 2, -2)[n]
        if n < 4:
            return remote(own, own, z_send.at[n], line_recv.at[0, OFFSETS.index(-d)], along_z[d])
        came = -2 if d > 0 else 2
        ref = block(0, OFFSETS.index(came))
        if n < 6:
            return remote(ref, ref, z_send.at[n], line_recv.at[0, OFFSETS.index(came - d)], along_z[d])
        ref = ref.at[pl.ds(0, HALF)] if d > 0 else ref.at[pl.ds(HALF, BLOCK - HALF)]
        return remote(ref, ref, z_send.at[n], half_recv.at[n - 6], along_z[d])

    def column_copy(n):
        d = (1, -1)[n % 2]
        ref = blocks.at[core, z, pl.ds(1, 2) if n < 2 else pl.ds(3, 1)]
        return remote(ref, ref, column_send.at[n], line_recv.at[1 if n < 2 else 3, OFFSETS.index(-d)], along_z[d])

    def partner_copy(e):
        return remote(block(0, e), block(2, e), partner_send.at[e], line_recv.at[2, e], partner)

    def near_copy(e):
        return remote(block(0, e), block(1, e), near_send.at[e], line_recv.at[1, e], near_before)

    far_to = tuple(jnp.where(core == 0, p, n) for p, n in zip(partner, near_before))

    def far_copy(e):
        if e in DIRECT:
            return remote(block(0, e), block(3, e), far_send.at[e], line_recv.at[3, e], far_before)
        return remote(block(1 + core, e), block(3, e), far_send.at[e], line_recv.at[3, e], far_to)

    def sib_copy(part, e, core_=None):
        first, count = ((0, 1), (1, 2), (3, 1))[part]
        ref = blocks.at[core if core_ is None else core_, spot(OFFSETS[e]), pl.ds(first, count)]
        return remote(ref, ref, sib_send.at[part, e], sib_recv.at[part, e], sibling)

    def arrived(line_, e):
        if line_ == 0 and e == 7:
            for n in range(2):
                z_copy(6 + n).wait_recv()
            return
        ref = block(line_, e)
        if line_ == 1 and e in (1, 2):
            ref = blocks.at[core, spot(OFFSETS[e]), pl.ds(1, 2)]
        remote(ref, ref, z_send.at[0], line_recv.at[line_, e], sibling).wait_recv()

    def pass_on(e):
        if e > 0:
            arrived(0, e)
        if e == 4:
            z_copy(4).start()
            z_copy(6).start()
        if e == 3:
            z_copy(5).start()
            z_copy(7).start()
        if e not in (1, 2):
            partner_copy(e).start()
            near_copy(e).start()
            if e in DIRECT:
                far_copy(e).start()
        sib_copy(0, e).start()

    def pass_far(e):
        arrived(1, e)
        if e not in (1, 2):
            arrived(2, e)
            if e not in DIRECT:
                far_copy(e).start()
        if e == 0:
            column_copy(0).start()
            column_copy(1).start()
        sib_copy(1, e).start()

    def pass_last(e):
        arrived(3, e)
        if e == 0:
            column_copy(2).start()
            column_copy(3).start()
        sib_copy(2, e).start()

    def from_sibling(part, e):
        sib_copy(part, e, 1 - core).wait_recv()

    def need(messages):
        for part, e in messages:
            from_sibling(part, e)

    for n in (0, 1):
        z_copy(n).start()
    pass_on(0)
    send_places = remote(place_out, place_in, q_send.at[0], q_recv.at[0], queries_to)
    send_queries = remote(queries.at[0], queries.at[1], q_send.at[1], q_recv.at[1], queries_to)
    for n in (2, 3):
        z_copy(n).start()
    send_places.start()
    send_queries.start()
    pass_far(0)
    pass_on(1)
    pass_on(2)

    def attend(which, spots):
        parts = [blocks.at[c, zz, j] for c, zz, j in spots]
        count = len(parts)
        keys = jnp.concatenate([part[0:HD, :] for part in parts], axis=1)
        values = jnp.concatenate([part[HD : 2 * HD, :] for part in parts], axis=0)
        values = jnp.concatenate([values, jnp.ones((count * TOK, HD), BF16)], axis=1)
        own_place = places[which]
        bias = []
        for part in parts:
            key_place = part[2 * HD : 2 * HD + 1, :].astype(F32) * 256.0 + part[2 * HD + 1 : 2 * HD + 2, :].astype(F32)
            bias.append(jnp.where(key_place <= own_place, 0.0, HIDDEN).astype(BF16))
        keys = jnp.concatenate([keys, jnp.concatenate(bias, axis=1)], axis=0)
        for head in range(HEADS):
            rows = pl.ds(head * TOK, TOK)
            left = jnp.concatenate([queries[which, :, head * HD : (head + 1) * HD], eye[...]], axis=1)
            scores = jnp.dot(left, keys, preferred_element_type=F32)
            most = scores[:, 0:TOK]
            for i in range(1, count):
                most = jnp.maximum(most, scores[:, i * TOK : (i + 1) * TOK])
            old = top[which, rows, :]
            new = jnp.maximum(old, jnp.max(most, axis=1, keepdims=True) * TO_LOG2)
            fade = jnp.exp2(old - new)
            top[which, rows, :] = new
            weights = jnp.concatenate(
                [jnp.exp2(scores[:, i * TOK : (i + 1) * TOK] * TO_LOG2 - new).astype(BF16) for i in range(count)],
                axis=1,
            )
            acc[which, rows, :] = acc[which, rows, :] * jnp.concatenate([fade, fade], axis=1) + jnp.dot(
                weights, values, preferred_element_type=F32
            )

    def back_copy(n):
        rows = pl.ds(n * BACK_ROWS, BACK_ROWS)
        return remote(part_out.at[rows], part_in.at[rows], back_send.at[n], back_recv.at[n], queries_from)

    lse_copy = remote(lse_out, lse_in, lse_send.at[0], lse_recv.at[0], queries_from)

    def early(i):
        if i == 1:
            pass_last(0)
            pass_on(3)
            pass_on(4)
            send_places.wait_recv()
            send_queries.wait_recv()
            got = place_in[...].astype(F32)
            places[1] = column_of(got[0:1, :] * 256.0 + got[1:2, :])
        elif i == 2:
            pass_far(1)
            pass_far(2)
            need(((0, 0), (0, 1), (1, 0)))
        elif i == 3:
            pass_on(5)
            pass_on(6)
            pass_last(1)
            pass_last(2)
        elif i == 4:
            pass_far(3)
            pass_far(4)
            pass_on(7)
            need(((0, 2), (2, 0), (1, 1), (1, 2), (0, 3), (0, 4)))
        elif i == 5:
            pass_far(5)
            pass_far(6)
        elif i == 6:
            pass_far(7)
            pass_last(3)
            pass_last(4)
            need(((2, 1), (2, 2), (1, 3), (1, 4), (0, 5), (0, 6)))
        elif i == 7:
            pass_last(5)
            pass_last(6)
            pass_last(7)
            need(((2, 3), (2, 4), (1, 5), (1, 6), (0, 7), (1, 7)))
        elif i == 8:
            need(((2, 7), (2, 5), (2, 6)))

    def give_back():
        for head in range(HEADS):
            rows = pl.ds(head * TOK, TOK)
            total = acc[1, rows, HD:]
            part_out[rows, :] = (acc[1, rows, 0:HD] / total).astype(BF16)
            if (head + 1) * TOK % BACK_ROWS == 0:
                back_copy((head + 1) * TOK // BACK_ROWS - 1).start()
            lse = top[1, rows, :] + jnp.log2(total)
            lse_out[head : head + 1, :] = jnp.sum(jnp.where(eye[...] != 0, lse, 0.0), axis=0, keepdims=True)
        lse_copy.start()

    def choose(index, tiles):
        found = []
        for choices in zip(*tiles):
            side, line_, e = choices[-1]
            distance = OFFSETS[e]
            for n in range(len(tiles) - 1):
                side = jnp.where(index == n, choices[n][0], side)
                line_ = jnp.where(index == n, choices[n][1], line_)
                distance = jnp.where(index == n, OFFSETS[choices[n][2]], distance)
            found.append((core + side - 2 * core * side, spot(distance), line_))
        return found

    def item(i, carry):
        other = (i == 1) | (i == 2) | (i == 4) | (i == 6) | (i == 7) | (i == 8)
        which = jnp.where(other, 1, 0)
        for n in range(1, 9):

            @pl.when(i == n)
            def _(n=n):
                early(n)

        small = (i < 2) | (i == 8) | (i == 11)
        middle = (i == 2) | (i == 3) | (i == 7) | (i == 10)

        @pl.when(small)
        def _():
            attend(which, choose(jnp.where(i < 2, 0, 1), SMALL))

        @pl.when(middle)
        def _():
            attend(which, choose(jnp.where(i < 4, 0, 1), MIDDLE))

        @pl.when(jnp.logical_not(small | middle))
        def _():
            attend(which, choose(jnp.where(i < 6, 0, 1), LARGE))

        @pl.when(i == 8)
        def _():
            give_back()

        return carry

    lax.fori_loop(0, ITEMS, item, 0)

    lse_copy.wait_recv()
    for head in range(HEADS):
        rows = pl.ds(head * TOK, TOK)
        if head * TOK % BACK_ROWS == 0:
            back_copy(head * TOK // BACK_ROWS).wait_recv()
        total = acc[0, rows, HD:]
        mine = top[0, rows, :] + jnp.log2(total)
        theirs = column_of(lse_in[head : head + 1, :])
        larger = jnp.maximum(mine, theirs)
        share, other_share = jnp.exp2(mine - larger), jnp.exp2(theirs - larger)
        both = share + other_share
        result = acc[0, rows, 0:HD] * (share / (total * both)) + part_in[rows, :].astype(F32) * (other_share / both)
        att_ref[:, head * HD : (head + 1) * HD] = result.astype(BF16)
        lse = (larger + jnp.log2(both)) * LN2
        log_ref[head : head + 1, :] = jnp.sum(jnp.where(eye[...] != 0, lse, 0.0), axis=0, keepdims=True)

    for n in range(8):
        z_copy(n).wait_send()
    for n in range(4):
        column_copy(n).wait_send()
    for e in range(NZ):
        if e not in (1, 2):
            partner_copy(e).wait_send()
            near_copy(e).wait_send()
            far_copy(e).wait_send()
        for part in range(3):
            sib_copy(part, e).wait_send()
    send_places.wait_send()
    send_queries.wait_send()
    for n in range(HEADS * TOK // BACK_ROWS):
        back_copy(n).wait_send()
    lse_copy.wait_send()


def local(queries, keys, values, positions):
    vmem = pl.BlockSpec(memory_space=pltpu.VMEM)
    hbm = pl.BlockSpec(memory_space=pltpu.HBM)
    dma = pltpu.SemaphoreType.DMA
    backs = HEADS * TOK // BACK_ROWS
    return pl.pallas_call(
        kernel,
        out_shape=(
            jax.ShapeDtypeStruct((TOK, HEADS * HD), BF16),
            jax.ShapeDtypeStruct((HEADS, TOK), F32),
        ),
        in_specs=[hbm] * 4,
        out_specs=(vmem, vmem),
        scratch_shapes=[
            pltpu.VMEM((2, NZ, 4, BLOCK, HD), BF16),
            pltpu.VMEM((2, TOK, HEADS * HD), BF16),
            pltpu.VMEM((TOK, HD), BF16),
            pltpu.VMEM((1, TOK), jnp.int32),
            pltpu.VMEM((2, TOK, TOK), F32),
            pltpu.VMEM((16, TOK), BF16),
            pltpu.VMEM((16, TOK), BF16),
            pltpu.VMEM((TOK, TOK), BF16),
            pltpu.VMEM((2, HEADS * TOK, 2 * HD), F32),
            pltpu.VMEM((2, HEADS * TOK, TOK), F32),
            pltpu.VMEM((HEADS * TOK, HD), BF16),
            pltpu.VMEM((HEADS * TOK, HD), BF16),
            pltpu.VMEM((HEADS, TOK), F32),
            pltpu.VMEM((HEADS, TOK), F32),
            dma((4,)), dma((8,)), dma((2,)), dma((4,)), dma((4, NZ)), dma((NZ,)), dma((NZ,)), dma((NZ,)), dma((3, NZ)), dma((3, NZ)),
            dma((2,)), dma((2,)), dma((backs,)), dma((backs,)), dma((1,)), dma((1,)),
        ],
        compiler_params=pltpu.CompilerParams(
            collective_id=0, has_side_effects=True, vmem_limit_bytes=63 * 2**20
        ),
    )(queries, keys, values, positions.reshape(1, TOK))


def solution(mesh):
    placed = (
        P(("row", "col"), None),
        P(("row", "col"), None),
        P(("row", "col"), None),
        P(("row", "col")),
    )
    return jax.shard_map(
        local,
        mesh=mesh,
        in_specs=placed,
        out_specs=(P(("row", "col"), None), P(None, ("row", "col"))),
        check_vma=False,
    )
```
